32 devices in a mesh: poles: 2 (over y), row: 4 (over z), col: 4 (over x, core).
Axes of the slice: x: 2, y: 2, z: 4, core: 2. Of those that a mesh axis runs over, the one named last changes fastest.
Arguments:
- root_inverse: float32 [16, 1024, 8, 1024], P('poles', 'row', None, 'col'), parts along dimension 0, may hold values from -6 to 6
- factor_panel: float32 [16, 1024, 2048], P('poles', 'col', 'row'), parts along dimension 0, may hold values from -0.0625 to 0.0625
- struct_mask: int32 [2, 32], replicated, may hold values 0 or 1
- child_diag_inverse: float32 [1024, 4096], P('row', ('poles', 'col')), parts along dimension 1, may hold values from -6 to 6
Outputs:
- panel_inverse: float32 [4096, 8, 1024], P(('poles', 'col'), None, 'row'), parts along dimension 0
- child_inverse: float32 [1024, 4096], P('row', ('poles', 'col')), parts along dimension 1
The draws below stay inside these ranges and needn't reach their ends.
There are 2 independent parts, one for each index of `poles`. The reference program is written for one: setup_inputs(seed, part) draws one part's arguments, and reference() takes and returns one part's arrays. A program takes and returns all parts, laid end to end along the dimension named above; an argument that names none is the same for every part. Nothing has to cross between parts.
All inputs are finite; a program needn't handle non-finite values.
Results may differ from the reference program's by a relative error of at most 0.0001.
Values sent between devices are 32-bit elements; how exact they have to be, the bound alone decides.
A program may use at most 192 MiB of HBM per device.

```python
import jax
import jax.numpy as jnp
from jax import lax

B = 256
W = 1024
NCH = 2
NBR = 32
N_ROW = 4
N_COL = 4


def place_ends(drawn, stream_key, least, largest):
    shape = drawn.shape
    spot = [jax.random.randint(jax.random.fold_in(stream_key, axis), (), 0, shape[axis]) for axis in range(len(shape))]
    drawn = drawn.at[tuple(spot)].set(least)
    longest = shape.index(max(shape))
    spot[longest] = (spot[longest] + 1) % shape[longest]
    return drawn.at[tuple(spot)].set(largest)


def steps_of(stream_key, extent, shards, low, top_value):
    factor_of = 1.0
    for dim, parts in shards:
        draws = jax.random.uniform(jax.random.fold_in(jax.random.fold_in(stream_key, 6), dim), (parts,), jnp.float32, low / len(shards), top_value / len(shards))
        factor_of = factor_of * jnp.repeat(jnp.exp(draws), extent[dim] // parts).reshape((-1,) + (1,) * (len(extent) - 1 - dim))
    return factor_of


def bell_draw(own_key, shape, scale, limit, split=(), kind=jnp.bfloat16):
    result = scale * jax.random.normal(own_key, shape, jnp.float32)
    if split:
        result = result * steps_of(own_key, shape, split, -0.22, 0.18)
    return jnp.clip(result, -limit, limit).astype(kind)


def setup_inputs(seed: int = 0, part: int = 0) -> dict:
    key_list = jax.random.split(jax.random.key(seed), 5)
    own_keys = jax.random.split(jax.random.fold_in(key_list[4], part), 5)
    root_inverse = bell_draw(own_keys[0], (NBR // N_ROW, N_ROW * B, NBR // N_COL, N_COL * B), 1.0, 6.0, ((1, 4), (3, 4)), jnp.float32)
    factor_panel = bell_draw(own_keys[1], (NBR // N_COL, N_COL * B, NCH * W), (NBR * B) ** -0.5, 0.0625, ((1, 4), (2, 4)), jnp.float32)
    struct_mask = place_ends((jax.random.randint(key_list[2], (NCH, NBR), 0, 3) < 2).astype(jnp.int32), jax.random.fold_in(key_list[2], 1), 0, 1)
    child_diag_inverse = bell_draw(own_keys[3], (W, NCH * W), 1.0, 6.0, ((0, 4), (1, 4)), jnp.float32)
    return dict(root_inverse=root_inverse, factor_panel=factor_panel, struct_mask=struct_mask, child_diag_inverse=child_diag_inverse)


def reference(root_inverse, factor_panel, struct_mask, child_diag_inverse):
    order = NBR * B
    total = NCH * W
    matrix = root_inverse.reshape(order, order)
    panel = factor_panel.reshape(order, total)
    mask_float = struct_mask.astype(jnp.float32).T
    spread = jnp.repeat(jnp.repeat(mask_float, B, axis=0), W, axis=1)
    masked = panel * spread
    product = jnp.dot(matrix, masked, precision=lax.Precision.HIGHEST)
    upper = -(product * spread)
    panel_inverse = upper.T.reshape(total, NBR // N_ROW, N_ROW * B)
    blocks = []
    for child_slot in range(NCH):
        left_part = masked[:, child_slot * W:(child_slot + 1) * W]
        right_part = upper[:, child_slot * W:(child_slot + 1) * W]
        inner = jnp.dot(left_part.T, right_part, precision=lax.Precision.HIGHEST)
        blocks.append(child_diag_inverse[:, child_slot * W:(child_slot + 1) * W] - inner)
    child_inverse = jnp.concatenate(blocks, axis=1)
    return panel_inverse, child_inverse
```

```python
import functools

import jax
import jax.numpy as jnp
from jax import lax
from jax.experimental import pallas as pl
from jax.experimental.pallas import tpu as pltpu
from jax.sharding import PartitionSpec as P

CHUNK = 128


def halves(x):
    high = lax.reduce_precision(x, 8, 7)
    return high.astype(jnp.bfloat16), (x - high).astype(jnp.bfloat16)


def product_kernel(blocks, groups, mask_ref, panel_ref, high_ref, low_ref, out_ref, left_high, left_low):
    depth, chunk = panel_ref.shape[1:]
    width = depth // groups

    @pl.when(pl.program_id(0) == 0)
    def _():
        for b in range(blocks):
            for t in range(groups):
                span = slice(t * width, (t + 1) * width)
                x = (panel_ref[b, span, :] * mask_ref[b, t]).T
                high = x.astype(jnp.bfloat16)
                left_high[b * chunk : (b + 1) * chunk, span] = high
                low = x - high.astype(jnp.float32)
                left_low[b * chunk : (b + 1) * chunk, span] = low.astype(jnp.bfloat16)

    def dot(a, b):
        return lax.dot_general(a[...], b[...], (((1,), (1,)), ((), ())), preferred_element_type=jnp.float32)

    out_ref[...] = dot(left_high, high_ref) + (dot(left_high, low_ref) + dot(left_low, high_ref))


def block_product(mask, panel, high, low, first, order):
    blocks, depth, chunk = panel.shape
    tile = min(256, order)
    start = first // tile
    return pl.pallas_call(
        functools.partial(product_kernel, blocks, mask.shape[1]),
        grid=(order // tile,),
        out_shape=jax.ShapeDtypeStruct((blocks * chunk, order), jnp.float32),
        in_specs=[
            pl.BlockSpec(memory_space=pltpu.SMEM),
            pl.BlockSpec((blocks, depth, chunk), lambda i: (0, 0, 0)),
            pl.BlockSpec((tile, depth), lambda i: (start + i, 0)),
            pl.BlockSpec((tile, depth), lambda i: (start + i, 0)),
        ],
        out_specs=pl.BlockSpec((blocks * chunk, tile), lambda i: (0, i)),
        scratch_shapes=[pltpu.VMEM((blocks * chunk, depth), jnp.bfloat16)] * 2,
        compiler_params=pltpu.CompilerParams(vmem_limit_bytes=40 * 2**20),
        cost_estimate=pl.CostEstimate(
            flops=6 * blocks * chunk * depth * order,
            bytes_accessed=4 * (depth * order + blocks * chunk * (depth + order)),
            transcendentals=0,
        ),
    )(mask, panel, high, low)


def reduce_cols(partial):
    cols = lax.axis_size("col")
    col = lax.axis_index("col")
    pair = 2 if cols % 2 == 0 else 1
    far = cols // pair
    here, core = col // pair, col % pair
    part = partial.reshape((far, pair) + partial.shape[1:])
    if pair == 2:
        mine = lax.dynamic_index_in_dim(part, core, 1, False)
        other = lax.dynamic_index_in_dim(part, 1 - core, 1, False)
        swap = [(c, c ^ 1) for c in range(cols)]
        part = mine + lax.ppermute(other, "col", swap)
    else:
        part = part[:, 0]
    total = lax.dynamic_index_in_dim(part, here, 0, False)
    for step in range(1, far):
        send = lax.dynamic_index_in_dim(part, (here + step) % far, 0, False)
        pairs = [(c, ((c // pair + step) % far) * pair + c % pair) for c in range(cols)]
        total = total + lax.ppermute(send, "col", pairs)
    return total


def own_rows_of(panel, rows, cols, group):
    row, col = lax.axis_index("row"), lax.axis_index("col")
    slices = panel.reshape((cols, rows // cols) + panel.shape[1:])
    holder = row % cols
    kept = lax.dynamic_index_in_dim(slices, col, 0, False)
    kept = jnp.where(holder == col, kept, jnp.zeros_like(kept))
    for step in range(1, cols):
        send = lax.dynamic_index_in_dim(slices, (col + step) % cols, 0, False)
        pairs = [(r * cols + r % cols, r * cols + (r % cols + step) % cols) for r in range(rows)]
        kept = kept + lax.ppermute(send, ("row", "col"), pairs)
    found = [kept]
    for step in range(1, group):
        pairs = [(c, c // group * group + (c % group + step) % group) for c in range(cols)]
        found.append(lax.ppermute(kept, "col", pairs))
    found = jnp.stack(found)
    place = col % group
    return [lax.dynamic_index_in_dim(found, (place - p) % group, 0, False) for p in range(group)]


def local(root_inverse, factor_panel, struct_mask, child_diag_inverse):
    rows, cols = lax.axis_size("row"), lax.axis_size("col")
    row, col = lax.axis_index("row"), lax.axis_index("col")
    local_rows, width, local_cols, _ = root_inverse.shape
    rows_here, cols_here = local_rows * width, local_cols * width
    block = factor_panel.shape[2]
    total = block * rows
    children = struct_mask.shape[0]
    child_width = total // children
    slice_width = total // cols
    chunk = min(CHUNK, block)
    ratio = rows // cols
    mask = struct_mask.astype(jnp.float32)
    mask_cols = lax.dynamic_index_in_dim(mask.reshape(children, local_cols, cols), col, 2, False)
    mask_rows = lax.dynamic_index_in_dim(mask.reshape(children, local_rows, rows), row, 2, False)
    spread = jnp.repeat(mask_cols, rows // children, axis=0)
    child_here = col * slice_width // child_width
    own_mask = jnp.repeat(lax.dynamic_index_in_dim(mask_rows, child_here, 0, False), width)

    high, low = halves(root_inverse.reshape(rows_here, cols_here))
    uppers, lefts = [], []
    pieces_here = [factor_panel[:, :, first : first + chunk] for first in range(0, block, chunk)]
    pieces_here = list(lax.optimization_barrier(tuple(pieces_here)))
    following = lax.all_gather(pieces_here[0], "row", axis=0)
    following, high, low = lax.optimization_barrier((following, high, low))
    for step in range(len(pieces_here)):
        panel = following
        if step + 1 < len(pieces_here):
            panel, after = lax.optimization_barrier((panel, pieces_here[step + 1]))
            following = lax.all_gather(after, "row", axis=0)
        panel = panel.reshape(rows, cols_here, chunk)
        own = lax.dynamic_index_in_dim(
            panel.reshape(rows, local_rows, ratio, width, chunk), row // cols, 2, False
        )
        own = own_rows_of(own.reshape(rows, rows_here, chunk), rows, cols, cols // children)
        last = step + 1 == len(pieces_here)
        pieces = 2 if last and rows_here % 512 == 0 else 1
        height = rows_here // pieces
        found = []
        for first in range(0, rows_here, height):
            product = block_product(spread, panel, high, low, first, height)
            found.append(reduce_cols(product.reshape(cols, ratio, chunk, height)))
        uppers.append(-jnp.concatenate(found, axis=2) * own_mask)
        lefts.append(own)
        if not last:
            following, uppers[-1], lefts[-1] = lax.optimization_barrier((following, uppers[-1], lefts[-1]))
    upper = jnp.concatenate(uppers, axis=1).reshape(slice_width, rows_here)
    left = jnp.stack([jnp.concatenate(part, axis=0) for part in lefts], axis=1)
    left_mask = lax.dynamic_index_in_dim(mask_rows, child_here, 0, True)
    left_mask = jnp.repeat(left_mask, left.shape[0] * left.shape[1], axis=0)
    left = left.reshape(-1, rows_here, chunk)
    partial = block_product(left_mask, left, *halves(upper), 0, slice_width)
    reduced = lax.psum_scatter(partial, "row", scatter_dimension=0, tiled=True)
    return (upper.reshape(slice_width, local_rows, width), child_diag_inverse - reduced)


def solution(mesh):
    return jax.shard_map(
        local,
        mesh=mesh,
        in_specs=(
            P("poles", "row", None, "col"),
            P("poles", "col", "row"),
            P(),
            P("row", ("poles", "col")),
        ),
        out_specs=(P(("poles", "col"), None, "row"), P("row", ("poles", "col"))),
        check_vma=False,
    )
```
